32 devices in a mesh: seq: 8 (over y, x, core), col: 4 (over z).
Axes of the slice: x: 2, y: 2, z: 4, core: 2. Of those that a mesh axis runs over, the one named last changes fastest.
Arguments:
- atoms: bfloat16 [4096, 128], P(('seq', 'col')), may hold values from -6 to 6
- cotangent: bfloat16 [4096, 128], P(('seq', 'col')), may hold values from -6 to 6
- token_counts: int32 [32, 16], replicated, may hold values from 1 to 24, 128 in all within a row
- pair: bfloat16 [512, 512, 128], P('seq', 'col'), may hold values from -450 to 450
- w_qkvg: bfloat16 [3, 128, 512], replicated, may hold values from -0.5 to 0.5
- w_out: bfloat16 [3, 128, 128], replicated, may hold values from -0.5 to 0.5
- w_up: bfloat16 [3, 128, 512], replicated, may hold values from -0.5 to 0.5
- w_down: bfloat16 [3, 256, 128], replicated, may hold values from -0.375 to 0.375
- w_pair: bfloat16 [128, 12], replicated, may hold values from -2 to 2
Outputs:
- out_atoms: bfloat16 [4096, 128], P(('seq', 'col'))
- grad_atoms: bfloat16 [4096, 128], P(('seq', 'col'))
- grad_pair: bfloat16 [512, 512, 128], P('seq', 'col')
- grad_qkvg: float32 [3, 128, 512], replicated
- grad_out: float32 [3, 128, 128], replicated
- grad_up: float32 [3, 128, 512], replicated
- grad_down: float32 [3, 256, 128], replicated
- grad_pair_w: float32 [128, 12], replicated
The draws below stay inside these ranges and needn't reach their ends.
Inputs may be any that keep to these rules, and one draw needn't show every extreme that they name: `token_counts`: each row sums to 128.
All inputs are finite; a program needn't handle non-finite values.
Results may differ from the reference program's by a relative error of at most 0.03.
Values may be sent and summed in bfloat16 or wider, within the bound.
No kernel may reach another device: no remote copies, remote signals or barrier semaphores. Data moves between devices by JAX's collectives and lax.ppermute only.
A program may use at most 128 MiB of HBM per device.

```python
import math
import jax
import jax.numpy as jnp
import numpy as np
from jax import lax

D = 128
HEADS = 4
CPAIR = 128
FF = 256
LAYERS = 3
Q_BLOCK = 32
K_BLOCK = 128
HALO = 48
BLK_DEV = 4
ATOM_DEV = 128
TOK_DEV = 16
MOST = 24
ATOMS = 4096
NTOK = 512
N_SEQ = 8
N_COL = 4


def draw_pair(key, part):
    key = jax.random.fold_in(key, 7)
    normal_key = jax.random.fold_in(key, 0)
    values = jax.random.truncated_normal(normal_key, -6.0, 6.0, (NTOK, NTOK, CPAIR), jnp.float32) * 0.25
    return values.astype(jnp.bfloat16)


def steps_of(stream_key, dims, cuts, low, top_value):
    def one(dim, parts):
        draws = jax.random.uniform(jax.random.fold_in(jax.random.fold_in(stream_key, 6), dim), (parts,), jnp.float32, low / len(cuts), top_value / len(cuts))
        return jnp.repeat(jnp.exp(draws), dims[dim] // parts).reshape((-1,) + (1,) * (len(dims) - dim - 1))

    loudness = one(*cuts[0])
    for cut in cuts[1:]:
        loudness = loudness * one(*cut)
    return loudness


def split_up(amount, total, reach, skew):
    loads = [(1 << 20) // math.isqrt(rank ** skew) + 1 for rank in range(2, amount + 1)]
    surplus, counts = total - reach - (amount - 1), [1] * (amount - 1)
    while surplus > 0:
        candidates = [i for i in range(amount - 1) if counts[i] < reach]
        whole, budget = sum([loads[i] for i in candidates]), surplus
        for i in candidates:
            extra = min(reach - counts[i], max(1, budget * loads[i] // whole), surplus)
            counts[i] = counts[i] + extra
            surplus = surplus - extra
    return np.array([reach] + counts)


def uneven_parts(own_key, amount, total, bound, skew):
    if amount == 2:
        one = jax.random.randint(own_key, (), max(1, total - bound), min(bound, total - 1) + 1)
        return jnp.stack([one, total - one])
    sizes = jnp.asarray(split_up(amount, total, bound, skew), jnp.int32)
    couples = (amount - 1) // 2
    giver, sink = sizes[1:1 + 2 * couples:2], sizes[2:2 + 2 * couples:2]
    slack = jnp.minimum(giver - 1, bound - sink)
    moved = jax.random.randint(jax.random.fold_in(own_key, 1), (couples,), 0, 1 << 20) % (slack + 1)
    sizes = sizes.at[1:1 + 2 * couples:2].set(giver - moved).at[2:2 + 2 * couples:2].set(sink + moved)
    return sizes[jax.random.permutation(jax.random.fold_in(own_key, 2), amount)]


def scatter_about(rng, extent, scale, bound, pieces=(), held_as=jnp.bfloat16):
    level = steps_of(rng, extent, pieces, -0.22, 0.18) if pieces else 1.0
    values = jax.random.normal(rng, extent, jnp.float32) * scale * level
    return jnp.minimum(jnp.maximum(values, -bound), bound).astype(held_as)


def setup_inputs(seed: int = 0) -> dict:
    key_list = jax.random.split(jax.random.key(seed), 10)
    return {
        "atoms": scatter_about(key_list[0], (ATOMS, D), 1.0, 6.0, ((0, 32),)),
        "cotangent": scatter_about(key_list[1], (ATOMS, D), 1.0, 6.0, ((0, 32),)),
        "token_counts": jax.vmap(lambda own: uneven_parts(own, TOK_DEV, ATOM_DEV, MOST, 2))(jax.random.split(key_list[2], (N_SEQ * N_COL))).reshape((N_SEQ * N_COL, TOK_DEV)).astype(jnp.int32),
        "pair": draw_pair(jax.random.fold_in(key_list[9], 71), 0),
        "w_qkvg": scatter_about(key_list[4], (LAYERS, D, 4 * D), D ** -0.5, 0.5),
        "w_out": scatter_about(key_list[5], (LAYERS, D, D), D ** -0.5, 0.5),
        "w_up": scatter_about(key_list[6], (LAYERS, D, 2 * FF), D ** -0.5, 0.5),
        "w_down": scatter_about(key_list[7], (LAYERS, FF, D), FF ** -0.5, 0.375),
        "w_pair": scatter_about(key_list[8], (CPAIR, LAYERS * HEADS), (CPAIR // 16) ** -0.5, 2.0),
    }


def layer_norm(vector):
    average = lax.optimization_barrier(jnp.mean(vector, axis=-1, keepdims=True))
    centred = vector - average
    spread = lax.optimization_barrier(jnp.mean(centred * centred, axis=-1, keepdims=True))
    return centred * lax.rsqrt(spread + 1e-05)

def project(resid_in, offset, w_qkvg_l):
    normed = layer_norm(resid_in).astype(jnp.bfloat16)
    pre_act = jnp.dot(normed, w_qkvg_l, preferred_element_type=jnp.float32) + offset
    feature_width = resid_in.shape[1]
    queries = pre_act[:, :feature_width].astype(jnp.bfloat16)
    key_value = pre_act[:, feature_width:3 * feature_width].astype(jnp.bfloat16)
    queries, key_value = lax.optimization_barrier((queries, key_value))
    gate_act = jax.nn.sigmoid(pre_act[:, 3 * feature_width:])
    return ((queries, key_value, gate_act), normed)

def attend(queries, windows, bias, key_valid):
    blocks = windows.shape[0]
    head_count = bias.shape[1]
    feature_width = queries.shape[1]
    head_dim = feature_width // head_count
    query_part = queries.astype(jnp.bfloat16).astype(jnp.float32).reshape(blocks, Q_BLOCK, head_count, head_dim)
    window_half = windows.astype(jnp.bfloat16).astype(jnp.float32)
    key_part = window_half[:, :, :feature_width].reshape(blocks, K_BLOCK, head_count, head_dim)
    value_part = window_half[:, :, feature_width:].reshape(blocks, K_BLOCK, head_count, head_dim)
    scores = jnp.einsum('bihd,bkhd->bhik', query_part, key_part, preferred_element_type=jnp.float32)
    scores = scores * (1.0 / math.sqrt(head_dim)) + bias
    scores = jnp.where(key_valid[:, None, None, :], scores, -1e+30)
    largest = lax.stop_gradient(lax.optimization_barrier(jnp.max(scores, axis=-1, keepdims=True)))
    weights = jnp.exp(scores - largest)
    weights = (weights / lax.optimization_barrier(jnp.sum(weights, axis=-1, keepdims=True))).astype(jnp.bfloat16)
    mixed = jnp.einsum('bhik,bkhd->bihd', weights.astype(jnp.float32), value_part, preferred_element_type=jnp.float32)
    return mixed.reshape(blocks * Q_BLOCK, feature_width)

def finish(mixed, gate_act, resid_in, offsets, w_out_l, w_up_l, w_down_l):
    hidden_width = w_down_l.shape[0]
    gated = (mixed * gate_act).astype(jnp.bfloat16)
    attn_sum = jnp.dot(gated, w_out_l, preferred_element_type=jnp.float32) + offsets[1]
    residual = resid_in + attn_sum
    normed_two = layer_norm(residual).astype(jnp.bfloat16)
    up_both = jnp.dot(normed_two, w_up_l, preferred_element_type=jnp.float32) + offsets[2]
    hidden = (jax.nn.silu(up_both[:, :hidden_width]) * up_both[:, hidden_width:]).astype(jnp.bfloat16)
    result = residual + jnp.dot(hidden, w_down_l, preferred_element_type=jnp.float32) + offsets[3]
    return (result.astype(jnp.bfloat16), (gated, normed_two, hidden))

def layer_global(current, bias, key_valid, offsets, w_qkvg_l, w_out_l, w_up_l, w_down_l):
    resid_in = current.astype(jnp.float32)
    (queries, key_value, gate_act), normed = project(resid_in, offsets[0], w_qkvg_l)
    padded = jnp.pad(key_value.astype(jnp.float32), ((HALO, HALO), (0, 0)))
    blocks = bias.shape[0]
    window_index = jnp.arange(blocks, dtype=jnp.int32)[:, None] * Q_BLOCK + jnp.arange(K_BLOCK, dtype=jnp.int32)[None, :]
    windows = padded[window_index]
    mixed = attend(queries.astype(jnp.float32), windows, bias, key_valid)
    result, (gated, normed_two, hidden) = finish(mixed, gate_act, resid_in, offsets, w_out_l, w_up_l, w_down_l)
    return (result, (normed, gated, normed_two, hidden))

def pick_table(table, query_rows, key_cols):
    return table[:, query_rows[:, None], key_cols[None, :]]

def outer_sum(left, right):
    return jnp.dot(left.astype(jnp.float32).T, right, precision=lax.Precision.HIGHEST)

def reference(atoms, cotangent, token_counts, pair, w_qkvg, w_out, w_up, w_down, w_pair):
    groups = N_SEQ * N_COL
    blocks = ATOMS // Q_BLOCK
    token_ends = jnp.cumsum(token_counts, axis=1).astype(jnp.int32)
    position = jnp.arange(ATOM_DEV, dtype=jnp.int32)
    local_token = lax.optimization_barrier(jnp.sum((token_ends[:, None, :] <= position[None, :, None]).astype(jnp.int32), axis=2)).astype(jnp.int32)
    global_token = (local_token + TOK_DEV * jnp.arange(groups, dtype=jnp.int32)[:, None]).reshape(ATOMS)
    block_group = jnp.arange(blocks, dtype=jnp.int32) // BLK_DEV
    query_token = global_token.reshape(blocks, Q_BLOCK) - TOK_DEV * block_group[:, None]
    key_position = jnp.arange(blocks, dtype=jnp.int32)[:, None] * Q_BLOCK - HALO + jnp.arange(K_BLOCK, dtype=jnp.int32)[None, :]
    key_valid = (key_position >= 0) & (key_position < ATOMS)
    key_token = global_token[jnp.clip(key_position, 0, ATOMS - 1)] - TOK_DEV * (block_group[:, None] - 1)
    key_token = jnp.where(key_valid, key_token, 0).astype(jnp.int32)

    def pair_tile(group_index):
        row_block = lax.dynamic_slice_in_dim(pair, (group_index * TOK_DEV).astype(jnp.int32), TOK_DEV, 0)
        columns = group_index * TOK_DEV - TOK_DEV + jnp.arange(3 * TOK_DEV, dtype=jnp.int32)
        inside = (columns >= 0) & (columns < NTOK)
        taken = jnp.take(row_block, jnp.clip(columns, 0, NTOK - 1).astype(jnp.int32), axis=1)
        return jnp.where(inside[None, :, None], taken, jnp.zeros_like(taken))
    tiles_half = lax.map(pair_tile, jnp.arange(groups, dtype=jnp.int32))
    tiles = tiles_half.astype(jnp.float32)
    w_pair32 = w_pair.astype(jnp.float32)
    projected = jnp.einsum('gtuc,ch->ghtu', tiles, w_pair32, preferred_element_type=jnp.float32)
    zero_sets = []
    for layer_index in range(LAYERS):
        zero_sets.append((jnp.zeros((ATOMS, 4 * D), jnp.float32), jnp.zeros((ATOMS, D), jnp.float32), jnp.zeros((ATOMS, 2 * FF), jnp.float32), jnp.zeros((ATOMS, D), jnp.float32)))

    def forward(atoms_in, projected_in, offsets_all):
        per_block = projected_in[block_group]
        bias_all = jax.vmap(pick_table)(per_block, query_token, key_token)
        current = atoms_in
        saved = []
        for layer_index in range(LAYERS):
            bias = bias_all[:, layer_index * HEADS:(layer_index + 1) * HEADS]
            current, operands = layer_global(current, bias, key_valid, offsets_all[layer_index], w_qkvg[layer_index], w_out[layer_index], w_up[layer_index], w_down[layer_index])
            saved.append(operands)
            if layer_index + 1 < LAYERS:
                current = lax.optimization_barrier(current)
        return (current, saved)
    output, pullback, saved = jax.vjp(forward, atoms, projected, zero_sets, has_aux=True)
    grad_atoms, grad_projected, grad_offsets = pullback(cotangent)
    scale = 1.0 / math.sqrt(ATOMS)
    grad_qkvg = jnp.stack([outer_sum(saved[i][0], grad_offsets[i][0]) for i in range(LAYERS)]) * scale
    grad_out = jnp.stack([outer_sum(saved[i][1], grad_offsets[i][1]) for i in range(LAYERS)]) * scale
    grad_up = jnp.stack([outer_sum(saved[i][2], grad_offsets[i][2]) for i in range(LAYERS)]) * scale
    grad_down = jnp.stack([outer_sum(saved[i][3], grad_offsets[i][3]) for i in range(LAYERS)]) * scale
    grad_pair_w = jnp.einsum('gtuc,ghtu->ch', tiles, grad_projected, precision=lax.Precision.HIGHEST) * scale
    grad_tiles = jnp.einsum('ghtu,ch->gtuc', grad_projected, w_pair32, precision=lax.Precision.HIGHEST).astype(jnp.bfloat16)

    def place_tile(tile_args):
        group_index, tile_grad = tile_args
        columns = jnp.arange(NTOK, dtype=jnp.int32) - (group_index * TOK_DEV - TOK_DEV)
        inside = (columns >= 0) & (columns < 3 * TOK_DEV)
        taken = jnp.take(tile_grad, jnp.clip(columns, 0, 3 * TOK_DEV - 1).astype(jnp.int32), axis=1)
        return jnp.where(inside[None, :, None], taken, jnp.zeros_like(taken))
    grad_pair = lax.map(place_tile, (jnp.arange(groups, dtype=jnp.int32), grad_tiles)).reshape(NTOK, NTOK, CPAIR)
    return (output, grad_atoms, grad_pair, grad_qkvg, grad_out, grad_up, grad_down, grad_pair_w)
```

```python
from functools import partial
import math

import jax
import jax.numpy as jnp
from jax import lax
from jax.experimental import pallas as pl
from jax.experimental.pallas import tpu as pltpu
from jax.sharding import PartitionSpec as P

Q_BLOCK = 32
K_BLOCK = 128
HALO = 48
END = 64
F32 = jnp.float32
BF16 = jnp.bfloat16
VMEM_LIMIT = 40 * 1024 * 1024

NT = (((1,), (1,)), ((), ()))
TN = (((0,), (0,)), ((), ()))


def mm(a, b):
    return jnp.dot(a, b, preferred_element_type=F32)


def mm_nt(a, b):
    return lax.dot_general(a, b, NT, preferred_element_type=F32)


def mm_tn(a, b):
    return lax.dot_general(a, b, TN, preferred_element_type=F32)


def iota(shape, dim):
    return lax.broadcasted_iota(jnp.int32, shape, dim)


def layer_norm(x):
    average = jnp.mean(x, axis=-1, keepdims=True)
    centred = x - average
    spread = jnp.mean(centred * centred, axis=-1, keepdims=True)
    rstd = lax.rsqrt(spread + 1e-05)
    return centred * rstd, rstd


def layer_norm_back(d_normed, xhat, rstd):
    mean_d = jnp.mean(d_normed, axis=-1, keepdims=True)
    mean_dx = jnp.mean(d_normed * xhat, axis=-1, keepdims=True)
    return rstd * (d_normed - mean_d - xhat * mean_dx)


def head_mask(heads, feat):
    rows = heads * Q_BLOCK
    dim = feat // heads
    return (iota((rows, feat), 0) // Q_BLOCK == iota((rows, feat), 1) // dim).astype(F32)


def spread_heads(block, mask16, heads):
    return jnp.concatenate([block] * heads, axis=0) * mask16


def fold_heads(stacked, mask, heads):
    picked = stacked * mask
    total = picked[:Q_BLOCK]
    for h in range(1, heads):
        total = total + picked[h * Q_BLOCK : (h + 1) * Q_BLOCK]
    return total


def attend_block(q, k_win, v_win, hot, tsel, valid, mask, mask16, heads, scale):
    q_bd = spread_heads(q, mask16, heads)
    scores = mm_nt(q_bd, k_win) * scale + mm_nt(hot, tsel)
    scores = jnp.where(valid, scores, -1e30)
    expd = jnp.exp(scores - jnp.max(scores, axis=-1, keepdims=True))
    weights = (expd * (1.0 / jnp.sum(expd, axis=-1, keepdims=True))).astype(BF16)
    return weights, fold_heads(mm(weights, v_win), mask, heads)


def attend_block_back(d_mixed16, q, k_win, v_win, w16, mask, mask16, heads, scale):
    q_bd = spread_heads(q, mask16, heads)
    d_o = spread_heads(d_mixed16, mask16, heads)
    w32 = w16.astype(F32)
    d_w = mm_nt(d_o, v_win)
    delta = jnp.sum(d_w * w32, axis=-1, keepdims=True)
    d_s = (w32 * (d_w - delta)).astype(BF16)
    d_q = fold_heads(mm(d_s, k_win), mask, heads) * scale
    return d_s, d_q, mm_tn(d_s, q_bd) * scale, mm_tn(w16, d_o)


def finish(x16, mixed, gate, w_out, w_up, w_down):
    hidden_width = w_down.shape[0]
    gated = (mixed * gate).astype(BF16)
    residual = x16.astype(F32) + mm(gated, w_out)
    normed_two = layer_norm(residual)[0].astype(BF16)
    up = mm(normed_two, w_up)
    hidden = (jax.nn.silu(up[:, :hidden_width]) * up[:, hidden_width:]).astype(BF16)
    result = (residual + mm(hidden, w_down)).astype(BF16)
    return residual, up, result


def put_columns(ref, row, grad):
    height = grad.shape[0]
    for c in range(grad.shape[1] // 128):
        ref[row + c * height : row + (c + 1) * height, :] = grad[:, c * 128 : (c + 1) * 128].astype(BF16)
    return row + grad.shape[0] * (grad.shape[1] // 128)


def finish_back(d_result16, mixed, gate, residual, up, w_out, w_up, w_down):
    hidden_width = w_down.shape[0]
    xhat, rstd = layer_norm(residual)
    normed_two = xhat.astype(BF16)
    first, second = up[:, :hidden_width], up[:, hidden_width:]
    sig = jax.nn.sigmoid(first)
    act = first * sig
    hidden = (act * second).astype(BF16)
    d_hidden = mm_nt(d_result16, w_down).astype(BF16).astype(F32)
    d_first = d_hidden * second * (sig + act * (1.0 - sig))
    d_second = d_hidden * act
    d_up = jnp.concatenate([d_first, d_second], axis=1).astype(BF16)
    d_normed_two = mm_nt(d_up, w_up).astype(BF16).astype(F32)
    d_residual = d_result16.astype(F32) + layer_norm_back(d_normed_two, xhat, rstd)
    d_res16 = d_residual.astype(BF16)
    gated = (mixed * gate).astype(BF16)
    d_gated = mm_nt(d_res16, w_out).astype(BF16).astype(F32)
    d_mixed = d_gated * gate
    d_gate_pre = d_gated * mixed * gate * (1.0 - gate)
    pairs = ((gated, d_res16), (normed_two, d_up), (hidden, d_result16))
    return d_residual, d_mixed.astype(BF16), d_gate_pre.astype(BF16), pairs


def project_back(d_residual, d_q, d_kv, d_gate_pre, x16, w_qkvg):
    xhat, rstd = layer_norm(x16.astype(F32))
    d_pre = jnp.concatenate([d_q, d_kv.astype(BF16), d_gate_pre], axis=1)
    d_normed = mm_nt(d_pre, w_qkvg).astype(BF16).astype(F32)
    d_x = d_residual + layer_norm_back(d_normed, xhat, rstd)
    return d_x.astype(BF16), (xhat.astype(BF16), d_pre)


def split_three(value):
    high = value.astype(BF16)
    rest = value - high.astype(F32)
    middle = rest.astype(BF16)
    low = (rest - middle.astype(F32)).astype(BF16)
    return high, middle, low


def prefix_rows(counts, sources, lanes, key):
    out = []
    for inclusive in (True, False):
        total = None
        for k, c in enumerate(counts):
            token = iota((sources, lanes), 0) + k * sources
            at = key(iota((sources, lanes), 1))
            chosen = (token <= at) if inclusive else (token < at)
            part = mm(c, chosen.astype(F32).astype(BF16))
            total = part if total is None else total + part
        out.append(total[0:1])
    return out


def pieces(radius, atom_dev):
    out = []
    start = -radius
    while start < atom_dev + radius:
        stop = min((start // atom_dev + 1) * atom_dev, atom_dev + radius)
        out.append((start, stop - start))
        start = stop
    return out


def reach(radii):
    out = list(radii)
    for l in reversed(range(len(radii) - 1)):
        out[l] = max(out[l], out[l + 1] + 64)
    return out


def prepare(counts_ref, group, groups, table_refs, work_ref, hot_ref, khot_ref, tsel_ref, heads, atom_dev):
    tok = counts_ref.shape[1]
    span = 3 * tok
    ext = atom_dev + 2 * HALO
    blocks = atom_dev // Q_BLOCK
    rows = heads * Q_BLOCK
    sides = len(table_refs) // 2
    layers = tsel_ref.shape[1]
    count = layers * heads
    per_layer = heads * tok

    def row_of(offset):
        index = jnp.clip(group + offset, 0, groups - 1)
        c = counts_ref[pl.ds(index, 1), :].astype(F32)
        return jnp.broadcast_to(c, (8, tok)).astype(BF16)

    counts = [row_of(offset) for offset in range(-sides - 1, sides + 2)]
    place_k = (iota((ext, span), 0) + (atom_dev - HALO)).astype(F32)
    lanes = 3 * per_layer
    row_i = iota((blocks * rows, lanes), 0)
    lane_i = iota((blocks * rows, lanes), 1)
    place_q = ((row_i // rows) * Q_BLOCK + row_i % Q_BLOCK).astype(F32)
    same = (row_i // Q_BLOCK) % heads == (lane_i // tok) % heads
    place_q = jnp.where(same, place_q, -1.0)
    for n, table_ref in enumerate(table_refs):
        ends, starts = prefix_rows(counts[n : n + 3], tok, span, lambda lane: lane)
        khot = ((place_k >= starts) & (place_k < ends)).astype(F32).astype(BF16)
        if n == sides:
            khot_ref[...] = khot
        ends, starts = prefix_rows(counts[n + 1 : n + 2], tok, lanes, lambda lane: lane % tok)
        hot_ref[n] = ((place_q >= starts) & (place_q < ends)).astype(F32).astype(BF16)
        flat = table_ref[...]
        for t in range(tok):
            work_ref[n, pl.ds(t, count, stride=tok), 0:span] = flat[:count, t * span : (t + 1) * span]
        for l in range(layers):
            parts = split_three(work_ref[n, l * per_layer : (l + 1) * per_layer, 0:span])
            tsel_ref[n, l] = mm_nt(khot, jnp.concatenate(parts, axis=0)).astype(BF16)


def split_pre(pre, feat):
    q = pre[:, :feat].astype(BF16)
    kv = pre[:, feat : 3 * feat].astype(BF16)
    gate = jax.nn.sigmoid(pre[:, 3 * feat :])
    return q, kv, gate


def body_kernel(*refs, groups, heads, radii, forward, counts):
    take = iter(refs)
    group_ref, counts_ref = next(take), next(take)
    table_refs = [next(take) for _ in range(counts[0])]
    x_refs = [next(take) for _ in range(counts[1])]
    cot_refs = [next(take) for _ in range(counts[2])]
    wq_ref, wo_ref, wu_ref, wd_ref = [next(take) for _ in range(4)]
    out_ref, grads_ref, flat_ref = [next(take) for _ in range(3)]
    open_end = radii[0] < 64
    if open_end:
        dres_out, dq_out, dg_out, center_ref, head_ref, tail_ref = [next(take) for _ in range(6)]
    else:
        dx_out = next(take)
    work_ref, hot_ref, khot_ref, tsel_ref, tables_ref, flat_work = [next(take) for _ in range(6)]
    layers = len(radii)
    saved = [[next(take) for _ in range(8)] for _ in range(layers)]
    cot_ref, = [next(take) for _ in range(1)]
    back = [[next(take) for _ in range(5)] for _ in range(layers)]

    group = group_ref[0]
    atom_dev, feat = out_ref.shape
    sides = counts[0] // 2
    rows = heads * Q_BLOCK
    scale = 1.0 / math.sqrt(feat // heads)
    mask = head_mask(heads, feat)
    mask16 = mask.astype(BF16)
    tok = counts_ref.shape[1]
    per_layer = heads * tok
    span = 3 * tok

    row = 0
    for ref in x_refs:
        saved[0][0][row : row + ref.shape[0], :] = ref[...]
        row += ref.shape[0]
    row = 0
    for ref in cot_refs:
        cot_ref[row : row + ref.shape[0], :] = ref[...]
        row += ref.shape[0]
    prepare(counts_ref, group, groups, table_refs, work_ref, hot_ref, khot_ref, tsel_ref, heads, atom_dev)

    def window_of(start, b):
        at = start + b * Q_BLOCK
        n = at // atom_dev + sides
        inner = at % atom_dev // Q_BLOCK
        return at, n, inner

    for l in range(layers):
        x_ref, q_ref, kv_ref, gate_ref, w_ref, mixed_ref, res_ref, up_ref = saved[l]
        radius = forward[l]
        base_x = (x_ref.shape[0] - atom_dev) // 2
        wq, wo, wu, wd = wq_ref[l], wo_ref[l], wu_ref[l], wd_ref[l]
        for start, size in pieces(radius, atom_dev):
            at = start + radius
            pre = mm(layer_norm(x_ref[base_x + start : base_x + start + size, :].astype(F32))[0].astype(BF16), wq)
            q, kv, gate = split_pre(pre, feat)
            q_ref[at : at + size, :] = q
            kv_ref[at + HALO : at + HALO + size, :] = kv
            gate_ref[at : at + size, :] = gate
        low = base_x - radius - HALO
        high = base_x + atom_dev + radius
        edges = jnp.concatenate([x_ref[low : low + HALO, :], x_ref[high : high + HALO, :]], axis=0)
        edges = mm(layer_norm(edges.astype(F32))[0].astype(BF16), wq[:, feat : 3 * feat]).astype(BF16)
        kv_ref[0:HALO, :] = edges[:HALO]
        kv_ref[HALO + atom_dev + 2 * radius :, :] = edges[HALO:]
        for start, size in pieces(radius, atom_dev):
            mixed = []
            for b in range(size // Q_BLOCK):
                at, n, inner = window_of(start, b)
                low = at + radius
                position = group * atom_dev + (at - HALO) + iota((1, K_BLOCK), 1)
                valid = (position >= 0) & (position < groups * atom_dev)
                weights, part = attend_block(
                    q_ref[low : low + Q_BLOCK, :],
                    kv_ref[low : low + K_BLOCK, :feat],
                    kv_ref[low : low + K_BLOCK, feat:],
                    hot_ref[n, inner * rows : (inner + 1) * rows, :],
                    tsel_ref[n, l, inner * Q_BLOCK : inner * Q_BLOCK + K_BLOCK, :],
                    valid, mask, mask16, heads, scale,
                )
                w_ref[low * heads : low * heads + rows, :] = weights
                mixed.append(part)
            mixed = jnp.concatenate(mixed, axis=0)
            at = start + radius
            residual, up, result = finish(
                x_ref[base_x + start : base_x + start + size, :], mixed, gate_ref[at : at + size, :], wo, wu, wd
            )
            mixed_ref[at : at + size, :] = mixed
            res_ref[at : at + size, :] = residual
            up_ref[at : at + size, :] = up
            if l + 1 < layers:
                saved[l + 1][0][at : at + size, :] = result
            elif start == 0:
                out_ref[...] = result

    d_ref = cot_ref
    row = 0
    for l in reversed(range(layers)):
        x_ref, q_ref, kv_ref, gate_ref, w_ref, mixed_ref, res_ref, up_ref = saved[l]
        dres_ref, dq_ref, dg_ref, dkv_ref, dx_ref = back[l]
        radius, wide = radii[l], forward[l]
        wq, wo, wu, wd = wq_ref[l], wo_ref[l], wu_ref[l], wd_ref[l]
        dkv_ref[...] = jnp.zeros_like(dkv_ref)
        d_table = None
        for start, size in pieces(radius, atom_dev):
            at, far = start + radius, start + wide
            d_residual, d_mixed16, d_gate_pre, pairs = finish_back(
                d_ref[at : at + size, :], mixed_ref[far : far + size, :], gate_ref[far : far + size, :],
                res_ref[far : far + size, :], up_ref[far : far + size, :], wo, wu, wd,
            )
            dres_ref[at : at + size, :] = d_residual
            dg_ref[at : at + size, :] = d_gate_pre
            if start == 0:
                for left, right in pairs:
                    row = put_columns(grads_ref, row, mm_tn(left, right))
            for b in range(size // Q_BLOCK):
                place, n, inner = window_of(start, b)
                low, near = place + wide, place + radius
                d_s, d_q, d_k, d_v = attend_block_back(
                    d_mixed16[b * Q_BLOCK : (b + 1) * Q_BLOCK],
                    q_ref[low : low + Q_BLOCK, :],
                    kv_ref[low : low + K_BLOCK, :feat],
                    kv_ref[low : low + K_BLOCK, feat:],
                    w_ref[low * heads : low * heads + rows, :],
                    mask, mask16, heads, scale,
                )
                dq_ref[near : near + Q_BLOCK, :] = d_q.astype(BF16)
                dkv_ref[near : near + K_BLOCK, :feat] += d_k
                dkv_ref[near : near + K_BLOCK, feat:] += d_v
                if n == sides:
                    by_token = mm(d_s, khot_ref[inner * Q_BLOCK : inner * Q_BLOCK + K_BLOCK, :]).astype(BF16)
                    part = mm_tn(hot_ref[n, inner * rows : (inner + 1) * rows, :per_layer], by_token)
                    d_table = part if d_table is None else d_table + part
        tables_ref[l * per_layer : (l + 1) * per_layer, 0:span] = d_table
        if l == 0 and open_end:
            dres_out[...] = dres_ref[radius : radius + atom_dev, :]
            dq_out[...] = dq_ref[radius : radius + atom_dev, :]
            dg_out[...] = dg_ref[radius : radius + atom_dev, :]
            center_ref[...] = dkv_ref[HALO + radius : HALO + radius + atom_dev, :]
            head_ref[...] = dkv_ref[radius : radius + HALO, :].astype(BF16)
            tail_ref[...] = dkv_ref[HALO + radius + atom_dev : 2 * HALO + radius + atom_dev, :].astype(BF16)
            continue
        lower = radii[l - 1] if l else 0
        base_x = (x_ref.shape[0] - atom_dev) // 2
        for start, size in pieces(lower, atom_dev):
            at = start + radius
            d_x, (normed, d_pre) = project_back(
                dres_ref[at : at + size, :], dq_ref[at : at + size, :],
                dkv_ref[at + HALO : at + HALO + size, :], dg_ref[at : at + size, :],
                x_ref[base_x + start : base_x + start + size, :], wq,
            )
            if l:
                dx_ref[start + lower : start + lower + size, :] = d_x
            else:
                dx_out[...] = d_x
            if start == 0:
                row = put_columns(grads_ref, row, mm_tn(normed, d_pre))
        d_ref = dx_ref
    if row < grads_ref.shape[0]:
        grads_ref[row:, :] = jnp.zeros((grads_ref.shape[0] - row, 128), BF16)
    flat_work[...] = jnp.zeros_like(flat_work)
    count = layers * heads
    for t in range(tok):
        flat_work[0:count, t * span : (t + 1) * span] = tables_ref[pl.ds(t, count, stride=tok), 0:span]
    flat_ref[...] = flat_work[...].astype(BF16)


def joined(center, prev, nxt):
    atom_dev, width = center.shape
    gap = jnp.zeros((atom_dev - HALO, width), F32)
    return (
        center
        + jnp.concatenate([prev.astype(F32), gap], axis=0)
        + jnp.concatenate([gap, nxt.astype(F32)], axis=0)
    )


def last_kernel(
    dres_ref, dq_ref, dg_ref, center_ref, prev_ref, next_ref, x_ref, wq_ref,
    dx_ref, grads_ref,
):
    d_kv = joined(center_ref[...], prev_ref[...], next_ref[...])
    d_x16, (normed, d_pre) = project_back(
        dres_ref[...], dq_ref[...], d_kv, dg_ref[...], x_ref[...], wq_ref[0]
    )
    put_columns(grads_ref, 0, mm_tn(normed, d_pre))
    dx_ref[...] = d_x16


def tile_copies(place_ref, pair_ref, tiles_ref, sem, tok, col_width):
    copies = []
    for j in range(tiles_ref.shape[0]):
        for u in range(3):
            at = place_ref[0] + (j - 1 + u) * tok
            at = pl.multiple_of(jnp.clip(at, 0, col_width - tok), tok)
            copies.append(
                pltpu.make_async_copy(
                    pair_ref.at[pl.ds(j * tok, tok), pl.ds(at, tok), :],
                    tiles_ref.at[j, :, pl.ds(u * tok, tok), :],
                    sem.at[j * 3 + u],
                )
            )
    return copies


def lanes_inside(place, j, tok, col_width):
    lane = iota((1, 3 * tok * tok), 1)
    local = place + (j - 1) * tok + lane % (3 * tok)
    return (local >= 0) & (local < col_width)


def pair_kernel(place_ref, pair_ref, wt_ref, tab_ref, tiles_ref, sem, *, tok):
    col_width = pair_ref.shape[1]
    copies = tile_copies(place_ref, pair_ref, tiles_ref, sem, tok, col_width)
    for copy in copies:
        copy.start()
    for copy in copies:
        copy.wait()
    wt = wt_ref[...]
    for j in range(tiles_ref.shape[0]):
        flat = tiles_ref[j].reshape(3 * tok * tok, tiles_ref.shape[3])
        table = mm_nt(wt, flat)
        tab_ref[j] = jnp.where(lanes_inside(place_ref[0], j, tok, col_width), table, 0.0)


def pair_back_kernel(
    place_ref, dts_ref, pair_ref, wt_ref, gp_ref, gw_ref, tiles_ref, sem, *, tok
):
    col_width = pair_ref.shape[1]
    copies = tile_copies(place_ref, pair_ref, tiles_ref, sem, tok, col_width)
    for copy in copies:
        copy.start()
    gp_ref[...] = jnp.zeros_like(gp_ref)
    for copy in copies:
        copy.wait()
    wt = wt_ref[...]
    channels = tiles_ref.shape[3]
    total = None
    for j in range(tiles_ref.shape[0]):
        flat = tiles_ref[j].reshape(3 * tok * tok, channels)
        inside = lanes_inside(place_ref[0], j, tok, col_width)
        dt = jnp.where(inside, dts_ref[j].astype(F32), 0.0).astype(BF16)
        part = mm(dt, flat)
        total = part if total is None else total + part
        tile = mm_tn(dt, wt).astype(BF16).reshape(tok, 3 * tok, channels)
        for u in range(3):
            at = place_ref[0] + (j - 1 + u) * tok

            @pl.when((at >= 0) & (at < col_width))
            def _():
                start = pl.multiple_of(at, tok)
                gp_ref[j * tok : (j + 1) * tok, pl.ds(start, tok), :] = tile[:, u * tok : (u + 1) * tok, :]

    gw_ref[...] = total.astype(BF16)


def unpack_kernel(rows_ref, q_ref, o_ref, u_ref, d_ref, w_ref, *, scale, height):
    layers = q_ref.shape[0]

    def read(start, stop):
        out = []
        while start < stop:
            part, at = divmod(start, height)
            count = min(stop - start, height - at)
            out.append(rows_ref[part, at : at + count, :])
            start += count
        return out[0] if len(out) == 1 else jnp.concatenate(out, axis=0)

    def take(ref, l, row):
        tall = ref.shape[1]
        for c in range(ref.shape[2] // 128):
            block = read(row + c * tall, row + (c + 1) * tall)
            ref[l, :, c * 128 : (c + 1) * 128] = block.astype(F32) * scale
        return row + tall * (ref.shape[2] // 128)

    row = 0
    for l in reversed(range(layers)):
        row = take(o_ref, l, row)
        row = take(u_ref, l, row)
        row = take(d_ref, l, row)
        row = take(q_ref, l, row)
    total = rows_ref[0, height:, :].astype(F32)
    for part in range(1, rows_ref.shape[0]):
        total = total + rows_ref[part, height:, :].astype(F32)
    w_ref[...] = total * scale


def spec():
    return pl.BlockSpec(memory_space=pltpu.VMEM)


SMEM = pl.BlockSpec(memory_space=pltpu.SMEM)
HBM = pl.BlockSpec(memory_space=pltpu.HBM)


def call(kernel, name, in_specs, out_shape, scratch, *args):
    return pl.pallas_call(
        kernel,
        name=name,
        in_specs=in_specs,
        out_shape=out_shape,
        out_specs=jax.tree.map(lambda _: spec(), out_shape),
        scratch_shapes=scratch,
        compiler_params=pltpu.CompilerParams(vmem_limit_bytes=VMEM_LIMIT),
    )(*args)


def shape(*dims, dtype=F32):
    return jax.ShapeDtypeStruct(dims, dtype)


def shifted(value, axes, count, by):
    if by > 0:
        perm = [(i, i + by) for i in range(count - by)]
    else:
        perm = [(i - by, i) for i in range(count + by)]
    return lax.ppermute(value, axes, perm)


def swap(value, axis):
    return lax.all_to_all(value, axis, 0, 0, tiled=False)


def spread(value, axis):
    count = lax.axis_size(axis)
    return lax.all_to_all(jnp.broadcast_to(value[None], (count,) + value.shape), axis, 0, 0, tiled=False)


def scattered_sum(rows):
    seq_count, col_count = lax.axis_size("seq"), lax.axis_size("col")
    height = rows.shape[0]
    parts = swap(rows.reshape(seq_count, height // seq_count, 128), "seq")
    part = jnp.sum(parts.astype(F32), axis=0).astype(BF16)
    parts = swap(part.reshape(col_count, height // (seq_count * col_count), 128), "col")
    return jnp.sum(parts.astype(F32), axis=0).astype(BF16)


def gathered(part, extra):
    height = part.shape[0]
    parts = spread(jnp.concatenate([part, extra], axis=0), "col")
    extra = jnp.sum(parts[:, height:].astype(F32), axis=0).astype(BF16)
    part = parts[:, :height].reshape(-1, 128)
    return spread(jnp.concatenate([part, extra], axis=0), "seq")


def per_device(atoms, cotangent, token_counts, pair, w_qkvg, w_out, w_up, w_down, w_pair):
    seq_count = lax.axis_size("seq")
    col_count = lax.axis_size("col")
    groups = seq_count * col_count
    axes = ("seq", "col")
    seq_index = lax.axis_index("seq")
    col_index = lax.axis_index("col")
    group = (seq_index * col_count + col_index).astype(jnp.int32).reshape(1)
    atom_dev, feat = atoms.shape
    tok = token_counts.shape[1]
    layers = w_qkvg.shape[0]
    table_count = w_pair.shape[1]
    heads = table_count // layers
    hidden = w_down.shape[1]
    channels = pair.shape[2]
    col_width = pair.shape[1]
    ext = atom_dev + 2 * HALO
    span = 3 * tok
    rows = atom_dev * heads
    table_rows = -(-table_count // 16) * 16
    lanes = 3 * heads * tok
    radii = [END + 64 * l for l in range(layers)]
    forward = reach(radii)
    open_end = radii[0] < 64
    sides = -(-forward[0] // atom_dev)

    place = (seq_index * pair.shape[0] - col_index * col_width).astype(jnp.int32).reshape(1)
    wt = jnp.pad(w_pair.T, ((0, table_rows - table_count), (0, 0)))
    x_parts, cot_parts = [atoms], [cotangent]
    x_radius, cot_radius = forward[0] + HALO, radii[-1]
    for k in range(1, -(-x_radius // atom_dev) + 1):
        nx = min(atom_dev, x_radius - (k - 1) * atom_dev)
        nc = max(0, min(atom_dev, cot_radius - (k - 1) * atom_dev))
        up = shifted(jnp.concatenate([atoms[atom_dev - nx :], cotangent[atom_dev - nc :]], axis=0), axes, groups, k)
        down = shifted(jnp.concatenate([atoms[:nx], cotangent[:nc]], axis=0), axes, groups, -k)
        x_parts = [up[:nx]] + x_parts + [down[:nx]]
        if nc:
            cot_parts = [up[nx:]] + cot_parts + [down[nx:]]
    tile_scratch = [
        pltpu.VMEM((col_count, tok, span, channels), BF16),
        pltpu.SemaphoreType.DMA((col_count * 3,)),
    ]
    tables = call(
        partial(pair_kernel, tok=tok), "pair_tables", [SMEM, HBM, spec()],
        shape(col_count, table_rows, tok * span), tile_scratch, place, pair, wt,
    )
    table = jnp.sum(swap(tables, "col"), axis=0)
    tables = [table]
    for k in range(1, sides + 1):
        tables = [shifted(table, axes, groups, k)] + tables + [shifted(table, axes, groups, -k)]

    unit = 8 * groups
    rows_a = (feat * feat + 2 * feat * hidden + hidden * feat) // 128
    rows_q = 4 * feat * feat // 128
    grad_rows = layers * (rows_a + rows_q)
    padded = -(-grad_rows // unit) * unit
    out_shapes = [shape(atom_dev, feat, dtype=BF16)]
    if open_end:
        out_shapes += [shape(grad_rows - rows_q, 128, dtype=BF16)]
    else:
        out_shapes += [shape(padded, 128, dtype=BF16)]
    out_shapes += [shape(table_rows, tok * span, dtype=BF16)]
    if open_end:
        out_shapes += [
            shape(atom_dev, feat), shape(atom_dev, feat, dtype=BF16), shape(atom_dev, feat, dtype=BF16),
            shape(atom_dev, 2 * feat), shape(HALO, 2 * feat, dtype=BF16), shape(HALO, 2 * feat, dtype=BF16),
        ]
    else:
        out_shapes += [shape(atom_dev, feat, dtype=BF16)]
    scratch = [
        pltpu.VMEM((2 * sides + 1, table_count * tok, 128), F32),
        pltpu.VMEM((2 * sides + 1, rows, lanes), BF16),
        pltpu.VMEM((ext, span), BF16),
        pltpu.VMEM((2 * sides + 1, layers, ext, lanes), BF16),
        pltpu.VMEM((table_count * tok, 128), F32),
        pltpu.VMEM((table_rows, tok * span), F32),
    ]
    for l in range(layers):
        n = atom_dev + 2 * forward[l]
        nx = atom_dev + 2 * (forward[l - 1] if l else x_radius)
        scratch += [
            pltpu.VMEM((nx, feat), BF16), pltpu.VMEM((n, feat), BF16), pltpu.VMEM((n + 2 * HALO, 2 * feat), BF16),
            pltpu.VMEM((n, feat), F32), pltpu.VMEM((n * heads, K_BLOCK), BF16), pltpu.VMEM((n, feat), F32),
            pltpu.VMEM((n, feat), F32), pltpu.VMEM((n, 2 * hidden), F32),
        ]
    scratch += [pltpu.VMEM((atom_dev + 2 * cot_radius, feat), BF16)]
    for l in range(layers):
        n = atom_dev + 2 * radii[l]
        nx = atom_dev + 2 * (radii[l - 1] if l else 0)
        scratch += [
            pltpu.VMEM((n, feat), F32), pltpu.VMEM((n, feat), BF16), pltpu.VMEM((n, feat), BF16),
            pltpu.VMEM((n + 2 * HALO, 2 * feat), F32), pltpu.VMEM((nx, feat), BF16),
        ]
    args = [group, token_counts, *tables, *x_parts, *cot_parts, w_qkvg, w_out, w_up, w_down]
    results = call(
        partial(
            body_kernel, groups=groups, heads=heads, radii=radii, forward=forward,
            counts=(len(tables), len(x_parts), len(cot_parts)),
        ),
        "layers", [SMEM] + [spec()] * (len(args) - 1), out_shapes, scratch, *args,
    )
    out_atoms, grads, flat = results[:3]
    if open_end:
        d_res, d_q, d_g, center, head, tail = results[3:]
        d_next, d_prev = shifted(head, axes, groups, -1), shifted(tail, axes, groups, 1)
    flats = spread(flat, "col")
    if open_end:
        grad_atoms, last = call(
            last_kernel, "project_last", [spec()] * 8,
            [shape(atom_dev, feat, dtype=BF16), shape(rows_q, 128, dtype=BF16)], [],
            d_res, d_q, d_g, center, d_prev, d_next, atoms, w_qkvg,
        )
        grads = jnp.concatenate([grads, last, jnp.zeros((padded - grad_rows, 128), BF16)], axis=0)
    else:
        grad_atoms = results[3]
    part = scattered_sum(grads)
    grad_pair, pair_w = call(
        partial(pair_back_kernel, tok=tok), "pair_grads", [SMEM, spec(), HBM, spec()],
        [shape(*pair.shape, dtype=BF16), shape(table_rows, channels, dtype=BF16)],
        tile_scratch, place, flats, pair, wt,
    )
    scale = 1.0 / math.sqrt(atom_dev * groups)
    totals = gathered(part, pair_w)
    *outs, grad_w = call(
        partial(unpack_kernel, scale=scale, height=padded // seq_count), "unpack", [spec()],
        [shape(*w.shape) for w in (w_qkvg, w_out, w_up, w_down)] + [shape(table_rows, channels)], [], totals,
    )
    return (out_atoms, grad_atoms, grad_pair, *outs, grad_w[:table_count].T)


def solution(mesh):
    return jax.shard_map(
        per_device,
        mesh=mesh,
        in_specs=(
            P(("seq", "col"), None),
            P(("seq", "col"), None),
            P(),
            P("seq", "col", None),
            P(),
            P(),
            P(),
            P(),
            P(),
        ),
        out_specs=(
            P(("seq", "col"), None),
            P(("seq", "col"), None),
            P("seq", "col", None),
            P(),
            P(),
            P(),
            P(),
            P(),
        ),
        check_vma=False,
    )
```

```python
from functools import partial
import math

import jax
import jax.numpy as jnp
from jax import lax
from jax.experimental import pallas as pl
from jax.experimental.pallas import tpu as pltpu
from jax.sharding import PartitionSpec as P

Q_BLOCK = 32
K_BLOCK = 128
HALO = 48
F32 = jnp.float32
BF16 = jnp.bfloat16
VMEM_LIMIT = 40 * 1024 * 1024
PAIR_LIMIT = 61 * 1024 * 1024 + 512 * 1024

NT = (((1,), (1,)), ((), ()))
TN = (((0,), (0,)), ((), ()))


def mm(a, b):
    return jnp.dot(a, b, preferred_element_type=F32)


def mm_nt(a, b):
    return lax.dot_general(a, b, NT, preferred_element_type=F32)


def mm_tn(a, b):
    return lax.dot_general(a, b, TN, preferred_element_type=F32)


def iota(shape, dim):
    return lax.broadcasted_iota(jnp.int32, shape, dim)


def layer_norm(x):
    average = jnp.mean(x, axis=-1, keepdims=True)
    centred = x - average
    spread = jnp.mean(centred * centred, axis=-1, keepdims=True)
    rstd = lax.rsqrt(spread + 1e-05)
    return centred * rstd, rstd


def layer_norm_back(d_normed, xhat, rstd):
    mean_d = jnp.mean(d_normed, axis=-1, keepdims=True)
    mean_dx = jnp.mean(d_normed * xhat, axis=-1, keepdims=True)
    return rstd * (d_normed - mean_d - xhat * mean_dx)


def head_mask(heads, feat):
    rows = heads * Q_BLOCK
    dim = feat // heads
    return (iota((rows, feat), 0) // Q_BLOCK == iota((rows, feat), 1) // dim).astype(F32)


def spread_heads(block, mask16, heads):
    return jnp.concatenate([block] * heads, axis=0) * mask16


def fold_heads(stacked, mask, heads):
    picked = stacked * mask
    total = picked[:Q_BLOCK]
    for h in range(1, heads):
        total = total + picked[h * Q_BLOCK : (h + 1) * Q_BLOCK]
    return total


def attend_block(q, k_win, v_win, hot, tsel, valid, mask, mask16, heads, scale):
    q_bd = spread_heads(q, mask16, heads)
    scores = mm_nt(q_bd, k_win) * scale + mm_nt(hot, tsel)
    scores = jnp.where(valid, scores, -1e30)
    expd = jnp.exp(scores - jnp.max(scores, axis=-1, keepdims=True))
    weights = (expd * (1.0 / jnp.sum(expd, axis=-1, keepdims=True))).astype(BF16)
    return weights, fold_heads(mm(weights, v_win), mask, heads)


def attend_block_back(d_mixed16, q, k_win, v_win, w16, mask, mask16, heads, scale):
    q_bd = spread_heads(q, mask16, heads)
    d_o = spread_heads(d_mixed16, mask16, heads)
    w32 = w16.astype(F32)
    d_w = mm_nt(d_o, v_win)
    delta = jnp.sum(d_w * w32, axis=-1, keepdims=True)
    d_s = (w32 * (d_w - delta)).astype(BF16)
    d_q = fold_heads(mm(d_s, k_win), mask, heads) * scale
    return d_s, d_q, mm_tn(d_s, q_bd) * scale, mm_tn(w16, d_o)


def finish(x16, mixed, gate, w_out, w_up, w_down):
    hidden_width = w_down.shape[0]
    gated = (mixed * gate).astype(BF16)
    residual = x16.astype(F32) + mm(gated, w_out)
    normed_two = layer_norm(residual)[0].astype(BF16)
    up = mm(normed_two, w_up)
    hidden = (jax.nn.silu(up[:, :hidden_width]) * up[:, hidden_width:]).astype(BF16)
    result = (residual + mm(hidden, w_down)).astype(BF16)
    return residual, up, result


def put_columns(ref, row, grad):
    height = grad.shape[0]
    for c in range(grad.shape[1] // 128):
        ref[row + c * height : row + (c + 1) * height, :] = grad[:, c * 128 : (c + 1) * 128].astype(BF16)
    return row + grad.shape[0] * (grad.shape[1] // 128)


def finish_back(d_result16, mixed, gate, residual, up, w_out, w_up, w_down):
    hidden_width = w_down.shape[0]
    xhat, rstd = layer_norm(residual)
    normed_two = xhat.astype(BF16)
    first, second = up[:, :hidden_width], up[:, hidden_width:]
    sig = jax.nn.sigmoid(first)
    act = first * sig
    hidden = (act * second).astype(BF16)
    d_hidden = mm_nt(d_result16, w_down).astype(BF16).astype(F32)
    d_first = d_hidden * second * (sig + act * (1.0 - sig))
    d_second = d_hidden * act
    d_up = jnp.concatenate([d_first, d_second], axis=1).astype(BF16)
    d_normed_two = mm_nt(d_up, w_up).astype(BF16).astype(F32)
    d_residual = d_result16.astype(F32) + layer_norm_back(d_normed_two, xhat, rstd)
    d_res16 = d_residual.astype(BF16)
    gated = (mixed * gate).astype(BF16)
    d_gated = mm_nt(d_res16, w_out).astype(BF16).astype(F32)
    d_mixed = d_gated * gate
    d_gate_pre = d_gated * mixed * gate * (1.0 - gate)
    pairs = ((gated, d_res16), (normed_two, d_up), (hidden, d_result16))
    return d_residual, d_mixed.astype(BF16), d_gate_pre.astype(BF16), pairs


def project_back(d_residual, d_q, d_kv, d_gate_pre, x16, w_qkvg):
    xhat, rstd = layer_norm(x16.astype(F32))
    d_pre = jnp.concatenate([d_q, d_kv.astype(BF16), d_gate_pre], axis=1)
    d_normed = mm_nt(d_pre, w_qkvg).astype(BF16).astype(F32)
    d_x = d_residual + layer_norm_back(d_normed, xhat, rstd)
    return d_x.astype(BF16), (xhat.astype(BF16), d_pre)


def split_three(value):
    high = value.astype(BF16)
    rest = value - high.astype(F32)
    middle = rest.astype(BF16)
    low = (rest - middle.astype(F32)).astype(BF16)
    return high, middle, low


def prefix_rows(counts, sources, lanes, key):
    out = []
    for inclusive in (True, False):
        total = None
        for k, c in enumerate(counts):
            token = iota((sources, lanes), 0) + k * sources
            at = key(iota((sources, lanes), 1))
            chosen = (token <= at) if inclusive else (token < at)
            part = mm(c, chosen.astype(F32).astype(BF16))
            total = part if total is None else total + part
        out.append(total[0:1])
    return out


def row_of(counts_ref, index):
    c = counts_ref[pl.ds(index, 1), :].astype(F32)
    return jnp.broadcast_to(c, (8, counts_ref.shape[1])).astype(BF16)


def split_pre(pre, feat):
    q = pre[:, :feat].astype(BF16)
    kv = pre[:, feat : 3 * feat].astype(BF16)
    gate = jax.nn.sigmoid(pre[:, 3 * feat :])
    return q, kv, gate


def project(x16, w_qkvg):
    return mm(layer_norm(x16.astype(F32))[0].astype(BF16), w_qkvg)


def place_edges(even, head, tail, to_a_ref, to_b_ref):
    @pl.when(even)
    def _():
        to_a_ref[...] = head
        to_b_ref[...] = tail

    @pl.when(jnp.logical_not(even))
    def _():
        to_a_ref[...] = tail
        to_b_ref[...] = head


def extend(even, center, from_a_ref, from_b_ref, ext_ref):
    size = center.shape[0]
    ext_ref[HALO : HALO + size, :] = center

    @pl.when(even)
    def _():
        ext_ref[0:HALO, :] = from_a_ref[...]
        ext_ref[HALO + size :, :] = from_b_ref[...]

    @pl.when(jnp.logical_not(even))
    def _():
        ext_ref[0:HALO, :] = from_b_ref[...]
        ext_ref[HALO + size :, :] = from_a_ref[...]


def join(even, center_ref, from_a_ref, from_b_ref, total_ref):
    size = center_ref.shape[0]
    total_ref[...] = center_ref[...]

    def add(prev_ref, next_ref):
        total_ref[0:HALO, :] += prev_ref[...].astype(F32)
        total_ref[size - HALO :, :] += next_ref[...].astype(F32)

    @pl.when(even)
    def _():
        add(from_a_ref, from_b_ref)

    @pl.when(jnp.logical_not(even))
    def _():
        add(from_b_ref, from_a_ref)


def is_even(group):
    return lax.rem(group, 2) == 0


def ready_kernel(
    group_ref, counts_ref, x_ref, wq_ref, hot_ref, khot_ref, q_ref, kv_ref, gate_ref, *, groups, heads
):
    group = group_ref[0]
    atom_dev, feat = x_ref.shape
    tok = counts_ref.shape[1]
    span = 3 * tok
    ext = atom_dev + 2 * HALO
    blocks = atom_dev // Q_BLOCK
    rows = heads * Q_BLOCK
    lanes = 3 * heads * tok
    counts = [row_of(counts_ref, jnp.clip(group + offset, 0, groups - 1)) for offset in (-1, 0, 1)]
    ends, starts = prefix_rows(counts, tok, span, lambda lane: lane)
    place = (iota((ext, span), 0) + (atom_dev - HALO)).astype(F32)
    khot_ref[...] = ((place >= starts) & (place < ends)).astype(F32).astype(BF16)
    ends, starts = prefix_rows(counts[1:2], tok, lanes, lambda lane: lane % tok)
    row_i = iota((blocks * rows, lanes), 0)
    lane_i = iota((blocks * rows, lanes), 1)
    place = ((row_i // rows) * Q_BLOCK + row_i % Q_BLOCK).astype(F32)
    same = (row_i // Q_BLOCK) % heads == (lane_i // tok) % heads
    hot_ref[...] = (same & (place >= starts) & (place < ends)).astype(F32).astype(BF16)
    q, kv, gate = split_pre(project(x_ref[...], wq_ref[0]), feat)
    q_ref[...] = q
    kv_ref[...] = kv
    gate_ref[...] = gate


def select_tables(tables_ref, khot_ref, work_ref, tsel_ref, heads, tok):
    span = 3 * tok
    layers = tsel_ref.shape[0]
    count = layers * heads
    per_layer = heads * tok
    khot = khot_ref[...]
    flat = tables_ref[0]
    for source in range(1, tables_ref.shape[0]):
        flat = flat + tables_ref[source]
    for t in range(tok):
        work_ref[pl.ds(t, count, stride=tok), 0:span] = flat[:count, t * span : (t + 1) * span]
    for l in range(layers):
        parts = split_three(work_ref[l * per_layer : (l + 1) * per_layer, 0:span])
        tsel_ref[l] = mm_nt(khot, jnp.concatenate(parts, axis=0)).astype(BF16)


def attend(q, kv_ref, hot_ref, tsel_ref, group, groups, heads, w_ref):
    atom_dev, feat = q.shape
    rows = heads * Q_BLOCK
    mask = head_mask(heads, feat)
    mask16 = mask.astype(BF16)
    scale = 1.0 / math.sqrt(feat // heads)
    mixed = []
    for b in range(atom_dev // Q_BLOCK):
        low, high = b * Q_BLOCK, b * Q_BLOCK + K_BLOCK
        position = group * atom_dev + (low - HALO) + iota((1, K_BLOCK), 1)
        valid = (position >= 0) & (position < groups * atom_dev)
        weights, part = attend_block(
            q[low : low + Q_BLOCK], kv_ref[low:high, :feat], kv_ref[low:high, feat:],
            hot_ref[b * rows : (b + 1) * rows, :], tsel_ref[low:high, :],
            valid, mask, mask16, heads, scale,
        )
        w_ref[b * rows : (b + 1) * rows, :] = weights
        mixed.append(part)
    return jnp.concatenate(mixed, axis=0)


def attend_back(d_mixed16, q, kv_ref, w_ref, hot_ref, khot_ref, heads, dkv_ref):
    atom_dev, feat = q.shape
    rows = heads * Q_BLOCK
    mask = head_mask(heads, feat)
    mask16 = mask.astype(BF16)
    scale = 1.0 / math.sqrt(feat // heads)
    per_layer = hot_ref.shape[1] // 3
    dkv_ref[...] = jnp.zeros_like(dkv_ref)
    d_queries = []
    d_table = None
    for b in range(atom_dev // Q_BLOCK):
        low, high = b * Q_BLOCK, b * Q_BLOCK + K_BLOCK
        d_s, d_q, d_k, d_v = attend_block_back(
            d_mixed16[low : low + Q_BLOCK], q[low : low + Q_BLOCK], kv_ref[low:high, :feat], kv_ref[low:high, feat:],
            w_ref[b * rows : (b + 1) * rows, :], mask, mask16, heads, scale,
        )
        d_queries.append(d_q)
        dkv_ref[low:high, :feat] += d_k
        dkv_ref[low:high, feat:] += d_v
        by_token = mm(d_s, khot_ref[low:high, :]).astype(BF16)
        part = mm_tn(hot_ref[b * rows : (b + 1) * rows, :per_layer], by_token)
        d_table = part if d_table is None else d_table + part
    return jnp.concatenate(d_queries, axis=0).astype(BF16), d_table


def run_layer(refs, l, heads, groups, group):
    x_ref, q_ref, gate_ref, kvx_ref, hot_ref, tsel, w_ref, mixed_ref, res_ref, up_ref, wo_ref, wu_ref, wd_ref = refs
    mixed = attend(q_ref[...], kvx_ref, hot_ref, tsel, group, groups, heads, w_ref)
    residual, up, result = finish(x_ref[...], mixed, gate_ref[...], wo_ref[l], wu_ref[l], wd_ref[l])
    mixed_ref[...] = mixed
    res_ref[...] = residual
    up_ref[...] = up
    return result


def emit_next(result, w_qkvg, even, x1_ref, q1_ref, kv1_ref, gate1_ref, to_a_ref, to_b_ref):
    atom_dev, feat = result.shape
    x1_ref[...] = result
    q1, kv1, gate1 = split_pre(project(result, w_qkvg), feat)
    q1_ref[...] = q1
    kv1_ref[...] = kv1
    gate1_ref[...] = gate1
    place_edges(even, kv1[:HALO], kv1[atom_dev - HALO :], to_a_ref, to_b_ref)


def first_kernel(
    group_ref, tables_ref, x_ref, q_ref, kv_ref, gate_ref, from_a_ref, from_b_ref, hot_ref, khot_ref,
    wq_ref, wo_ref, wu_ref, wd_ref,
    x1_ref, q1_ref, kv1_ref, gate1_ref, to_a_ref, to_b_ref,
    kvx_ref, w_ref, mixed_ref, res_ref, up_ref, tsel_ref, xx_ref, work_ref, *, groups, heads, tok,
):
    group = group_ref[0]
    even = is_even(group)
    atom_dev, feat = x_ref.shape
    extend(even, x_ref[...], from_a_ref, from_b_ref, xx_ref)
    sides = jnp.concatenate([xx_ref[0:HALO, :], xx_ref[HALO + atom_dev :, :]], axis=0)
    sides = project(sides, wq_ref[0, :, feat : 3 * feat]).astype(BF16)
    kvx_ref[0:HALO, :] = sides[:HALO]
    kvx_ref[HALO : HALO + atom_dev, :] = kv_ref[...]
    kvx_ref[HALO + atom_dev :, :] = sides[HALO:]
    select_tables(tables_ref, khot_ref, work_ref, tsel_ref, heads, tok)
    result = run_layer(
        (x_ref, q_ref, gate_ref, kvx_ref, hot_ref, tsel_ref.at[0], w_ref, mixed_ref, res_ref, up_ref,
         wo_ref, wu_ref, wd_ref), 0, heads, groups, group,
    )
    emit_next(result, wq_ref[1], even, x1_ref, q1_ref, kv1_ref, gate1_ref, to_a_ref, to_b_ref)


def middle_kernel(
    group_ref, x_ref, q_ref, kv_ref, gate_ref, from_a_ref, from_b_ref, hot_ref, tsel_ref,
    wq_ref, wo_ref, wu_ref, wd_ref,
    x1_ref, q1_ref, kv1_ref, gate1_ref, to_a_ref, to_b_ref,
    kvx_ref, w_ref, mixed_ref, res_ref, up_ref, *, groups, heads, l,
):
    group = group_ref[0]
    even = is_even(group)
    extend(even, kv_ref[...], from_a_ref, from_b_ref, kvx_ref)
    result = run_layer(
        (x_ref, q_ref, gate_ref, kvx_ref, hot_ref, tsel_ref.at[l], w_ref, mixed_ref, res_ref, up_ref,
         wo_ref, wu_ref, wd_ref), l, heads, groups, group,
    )
    emit_next(result, wq_ref[l + 1], even, x1_ref, q1_ref, kv1_ref, gate1_ref, to_a_ref, to_b_ref)


def layer_back(
    d_result16, q_ref, kvx_ref, w_ref, mixed_ref, gate_ref, res_ref, up_ref, hot_ref, khot_ref,
    wo_ref, wu_ref, wd_ref, l, heads, even, row,
    dres_ref, dq_ref, dg_ref, center_ref, to_a_ref, to_b_ref, grads_ref, dkv_ref,
):
    atom_dev = q_ref.shape[0]
    d_residual, d_mixed16, d_gate_pre, pairs = finish_back(
        d_result16, mixed_ref[...], gate_ref[...], res_ref[...], up_ref[...], wo_ref[l], wu_ref[l], wd_ref[l]
    )
    d_q, d_table = attend_back(d_mixed16, q_ref[...], kvx_ref, w_ref, hot_ref, khot_ref, heads, dkv_ref)
    dres_ref[...] = d_residual
    dq_ref[...] = d_q
    dg_ref[...] = d_gate_pre
    center_ref[...] = dkv_ref[HALO : HALO + atom_dev, :]
    place_edges(
        even, dkv_ref[0:HALO, :].astype(BF16), dkv_ref[HALO + atom_dev :, :].astype(BF16), to_a_ref, to_b_ref
    )
    for left, right in pairs:
        row = put_columns(grads_ref, row, mm_tn(left, right))
    return d_table, row


def turn_kernel(
    group_ref, x_ref, q_ref, kv_ref, gate_ref, from_a_ref, from_b_ref, hot_ref, khot_ref, tsel_ref, cot_ref,
    wo_ref, wu_ref, wd_ref,
    out_ref, dres_ref, dq_ref, dg_ref, center_ref, to_a_ref, to_b_ref, dt_ref, grads_ref,
    kvx_ref, w_ref, mixed_ref, res_ref, up_ref, dkv_ref, *, groups, heads, l, used,
):
    group = group_ref[0]
    even = is_even(group)
    extend(even, kv_ref[...], from_a_ref, from_b_ref, kvx_ref)
    out_ref[...] = run_layer(
        (x_ref, q_ref, gate_ref, kvx_ref, hot_ref, tsel_ref.at[l], w_ref, mixed_ref, res_ref, up_ref,
         wo_ref, wu_ref, wd_ref), l, heads, groups, group,
    )
    d_table, _ = layer_back(
        cot_ref[...], q_ref, kvx_ref, w_ref, mixed_ref, gate_ref, res_ref, up_ref, hot_ref, khot_ref,
        wo_ref, wu_ref, wd_ref, l, heads, even, 0,
        dres_ref, dq_ref, dg_ref, center_ref, to_a_ref, to_b_ref, grads_ref, dkv_ref,
    )
    dt_ref[...] = d_table
    if used < grads_ref.shape[0]:
        grads_ref[used:, :] = jnp.zeros((grads_ref.shape[0] - used, 128), BF16)


def back_kernel(*refs, heads, l, row, tok, above):
    take = iter(refs)
    group_ref = next(take)
    dres2_ref, dq2_ref, dg2_ref, center2_ref, from_a_ref, from_b_ref, x2_ref = [next(take) for _ in range(7)]
    q_ref, kvx_ref, w_ref, mixed_ref, gate_ref, res_ref, up_ref = [next(take) for _ in range(7)]
    hot_ref, khot_ref, wq_ref, wo_ref, wu_ref, wd_ref = [next(take) for _ in range(6)]
    dt_above = [next(take) for _ in range(above)]
    next(take)
    dres_ref, dq_ref, dg_ref, center_ref, to_a_ref, to_b_ref = [next(take) for _ in range(6)]
    dt_ref, grads_ref = next(take), next(take)
    dkv_ref, total_ref = next(take), next(take)
    even = is_even(group_ref[0])
    join(even, center2_ref, from_a_ref, from_b_ref, total_ref)
    d_x16, (normed, d_pre) = project_back(
        dres2_ref[...], dq2_ref[...], total_ref[...], dg2_ref[...], x2_ref[...], wq_ref[l + 1]
    )
    row = put_columns(grads_ref, row, mm_tn(normed, d_pre))
    d_table, row = layer_back(
        d_x16, q_ref, kvx_ref, w_ref, mixed_ref, gate_ref, res_ref, up_ref, hot_ref, khot_ref,
        wo_ref, wu_ref, wd_ref, l, heads, even, row,
        dres_ref, dq_ref, dg_ref, center_ref, to_a_ref, to_b_ref, grads_ref, dkv_ref,
    )
    if not above:
        dt_ref[...] = d_table
        return
    tables_ref, flat_ref = next(take), next(take)
    span = 3 * tok
    height = d_table.shape[0]
    tables_ref[0:height, 0:span] = d_table
    for n, ref in enumerate(dt_above):
        tables_ref[(n + 1) * height : (n + 2) * height, 0:span] = ref[...]
    count = tables_ref.shape[0] // tok
    flat_ref[...] = jnp.zeros_like(flat_ref)
    for t in range(tok):
        flat_ref[0:count, t * span : (t + 1) * span] = tables_ref[pl.ds(t, count, stride=tok), 0:span]
    dt_ref[...] = flat_ref[...].astype(BF16)


def last_kernel(
    group_ref, core_ref, dres_ref, dq_ref, dg_ref, center_ref, from_a_ref, from_b_ref, x_ref, wq_ref, held_ref,
    dx_ref, send_ref, grads_ref, total_ref, *, row,
):
    even = is_even(group_ref[0])
    join(even, center_ref, from_a_ref, from_b_ref, total_ref)
    d_x16, (normed, d_pre) = project_back(
        dres_ref[...], dq_ref[...], total_ref[...], dg_ref[...], x_ref[...], wq_ref[0]
    )
    dx_ref[...] = d_x16
    put_columns(grads_ref, row, mm_tn(normed, d_pre))
    half = send_ref.shape[0]
    other = pl.multiple_of((1 - core_ref[0]) * half, 16)
    send_ref[...] = grads_ref[pl.ds(other, half), :]


def pair_sum_kernel(core_ref, grads_ref, got_ref, out_ref):
    half, shard = got_ref.shape[0], out_ref.shape[1]
    for part in range(half // shard):
        at = pl.multiple_of(core_ref[0] * half + part * shard, 16)
        mine = grads_ref[pl.ds(at, shard), :].astype(F32)
        out_ref[part] = (mine + got_ref[part * shard : (part + 1) * shard, :].astype(F32)).astype(BF16)


def shard_sum_kernel(parts_ref, out_ref):
    total = parts_ref[0].astype(F32)
    for part in range(1, parts_ref.shape[0]):
        total = total + parts_ref[part].astype(F32)
    out_ref[...] = total.astype(BF16)


def tile_copies(place_ref, pair_ref, tiles_ref, sem, tok, col_width):
    copies = []
    for j in range(tiles_ref.shape[0]):
        for u in range(3):
            at = place_ref[0] + (j - 1 + u) * tok
            at = pl.multiple_of(jnp.clip(at, 0, col_width - tok), tok)
            copies.append(
                pltpu.make_async_copy(
                    pair_ref.at[pl.ds(j * tok, tok), pl.ds(at, tok), :],
                    tiles_ref.at[j, :, pl.ds(u * tok, tok), :],
                    sem.at[j * 3 + u],
                )
            )
    return copies


def lanes_inside(place, j, tok, col_width):
    lane = iota((1, 3 * tok * tok), 1)
    local = place + (j - 1) * tok + lane % (3 * tok)
    return (local >= 0) & (local < col_width)


def pair_kernel(place_ref, pair_ref, wt_ref, tab_ref, tiles_ref, sem, *, tok):
    col_width = pair_ref.shape[1]
    copies = tile_copies(place_ref, pair_ref, tiles_ref, sem, tok, col_width)
    for copy in copies:
        copy.start()
    for copy in copies:
        copy.wait()
    wt = wt_ref[...]
    for j in range(tiles_ref.shape[0]):
        flat = tiles_ref[j].reshape(3 * tok * tok, tiles_ref.shape[3])
        table = mm_nt(wt, flat)
        tab_ref[j] = jnp.where(lanes_inside(place_ref[0], j, tok, col_width), table, 0.0)


def pair_back_kernel(
    place_ref, dts_ref, pair_ref, wt_ref, gp_ref, gw_ref, tiles_ref, sem, *, tok
):
    col_width = pair_ref.shape[1]
    copies = tile_copies(place_ref, pair_ref, tiles_ref, sem, tok, col_width)
    for copy in copies:
        copy.start()
    gp_ref[...] = jnp.zeros_like(gp_ref)
    for copy in copies:
        copy.wait()
    wt = wt_ref[...]
    channels = tiles_ref.shape[3]
    total = None
    for j in range(tiles_ref.shape[0]):
        flat = tiles_ref[j].reshape(3 * tok * tok, channels)
        inside = lanes_inside(place_ref[0], j, tok, col_width)
        dt = jnp.where(inside, dts_ref[j].astype(F32), 0.0).astype(BF16)
        part = mm(dt, flat)
        total = part if total is None else total + part
        tile = mm_tn(dt, wt).astype(BF16).reshape(tok, 3 * tok, channels)
        for u in range(3):
            at = place_ref[0] + (j - 1 + u) * tok

            @pl.when((at >= 0) & (at < col_width))
            def _():
                start = pl.multiple_of(at, tok)
                gp_ref[j * tok : (j + 1) * tok, pl.ds(start, tok), :] = tile[:, u * tok : (u + 1) * tok, :]

    gw_ref[...] = total.astype(BF16)


def unpack_kernel(core_ref, mine_ref, other_ref, q_ref, o_ref, u_ref, d_ref, w_ref, *, scale, height):
    layers = q_ref.shape[0]
    parts = mine_ref.shape[0]
    first = core_ref[0] == 0

    def read(start, stop):
        out = []
        while start < stop:
            part, at = divmod(start, height)
            count = min(stop - start, height - at)
            half, part = divmod(part, parts)
            mine = mine_ref[part, at : at + count, :].astype(F32)
            other = other_ref[part, at : at + count, :].astype(F32)
            out.append(jnp.where(first, other, mine) if half else jnp.where(first, mine, other))
            start += count
        return out[0] if len(out) == 1 else jnp.concatenate(out, axis=0)

    def take(ref, l, row):
        tall = ref.shape[1]
        for c in range(ref.shape[2] // 128):
            block = read(row + c * tall, row + (c + 1) * tall)
            ref[l, :, c * 128 : (c + 1) * 128] = block * scale
        return row + tall * (ref.shape[2] // 128)

    row = 0
    for l in reversed(range(layers)):
        row = take(o_ref, l, row)
        row = take(u_ref, l, row)
        row = take(d_ref, l, row)
        row = take(q_ref, l, row)
    total = None
    for ref in (mine_ref, other_ref):
        for part in range(parts):
            value = ref[part, height:, :].astype(F32)
            total = value if total is None else total + value
    w_ref[...] = total[: w_ref.shape[0]] * scale


def spec():
    return pl.BlockSpec(memory_space=pltpu.VMEM)


SMEM = pl.BlockSpec(memory_space=pltpu.SMEM)
HBM = pl.BlockSpec(memory_space=pltpu.HBM)


def call(kernel, name, in_specs, out_shape, scratch, *args, aliases={}, vmem=VMEM_LIMIT):
    return pl.pallas_call(
        kernel,
        name=name,
        in_specs=in_specs,
        out_shape=out_shape,
        out_specs=jax.tree.map(lambda _: spec(), out_shape),
        scratch_shapes=scratch,
        input_output_aliases=aliases,
        compiler_params=pltpu.CompilerParams(vmem_limit_bytes=vmem),
    )(*args)


def shape(*dims, dtype=F32):
    return jax.ShapeDtypeStruct(dims, dtype)


def swapped(to_a, to_b, count):
    axes = ("seq", "col")
    pairs_a = [p for i in range(1, count - 1, 2) for p in ((i, i + 1), (i + 1, i))]
    pairs_b = [p for i in range(0, count, 2) for p in ((i, i + 1), (i + 1, i))]
    from_a = lax.ppermute(to_a, axes, pairs_a)
    from_b = lax.ppermute(to_b, axes, pairs_b)
    return from_a, from_b


def swap(value, axis, groups=None):
    return lax.all_to_all(value, axis, 0, 0, axis_index_groups=groups, tiled=False)


def spread(value, axis, groups=None):
    count = lax.axis_size(axis) if groups is None else len(groups[0])
    return swap(jnp.broadcast_to(value[None], (count,) + value.shape), axis, groups)


def per_device(atoms, cotangent, token_counts, pair, w_qkvg, w_out, w_up, w_down, w_pair):
    seq_count = lax.axis_size("seq")
    col_count = lax.axis_size("col")
    groups = seq_count * col_count
    axes = ("seq", "col")
    seq_index = lax.axis_index("seq")
    col_index = lax.axis_index("col")
    group = (seq_index * col_count + col_index).astype(jnp.int32).reshape(1)
    core = lax.rem(seq_index, 2).astype(jnp.int32).reshape(1)
    atom_dev, feat = atoms.shape
    tok = token_counts.shape[1]
    layers = w_qkvg.shape[0]
    table_count = w_pair.shape[1]
    heads = table_count // layers
    hidden = w_down.shape[1]
    channels = pair.shape[2]
    col_width = pair.shape[1]
    ext = atom_dev + 2 * HALO
    span = 3 * tok
    rows = atom_dev * heads
    table_rows = -(-table_count // 16) * 16
    lanes = 3 * heads * tok

    place = (seq_index * pair.shape[0] - col_index * col_width).astype(jnp.int32).reshape(1)
    wt = jnp.pad(w_pair.T, ((0, table_rows - table_count), (0, 0)))
    even = lax.rem(col_index, 2) == 0
    head, tail = atoms[:HALO], atoms[atom_dev - HALO :]
    from_a, from_b = swapped(jnp.where(even, head, tail), jnp.where(even, tail, head), groups)
    tile_scratch = [
        pltpu.VMEM((col_count, tok, span, channels), BF16),
        pltpu.SemaphoreType.DMA((col_count * 3,)),
    ]
    tables = call(
        partial(pair_kernel, tok=tok), "pair_tables", [SMEM, HBM, spec()],
        shape(col_count, table_rows, tok * span), tile_scratch, place, pair, wt, vmem=PAIR_LIMIT,
    )
    tables = swap(tables, "col")

    bf = partial(shape, dtype=BF16)
    project_shapes = [bf(atom_dev, feat), bf(atom_dev, 2 * feat), shape(atom_dev, feat)]
    edge_shapes = [bf(HALO, 2 * feat), bf(HALO, 2 * feat)]
    saved_shapes = [
        bf(ext, 2 * feat), bf(rows, K_BLOCK), shape(atom_dev, feat), shape(atom_dev, feat), shape(atom_dev, 2 * hidden)
    ]
    hot, khot, q, kv, gate = call(
        partial(ready_kernel, groups=groups, heads=heads), "ready", [SMEM] + [spec()] * 3,
        [bf(rows, lanes), bf(ext, span)] + project_shapes, [], group, token_counts, atoms, w_qkvg,
    )
    weights = (w_qkvg, w_out, w_up, w_down)
    x = atoms
    saved = []
    for l in range(layers - 1):
        out_shapes = [bf(atom_dev, feat)] + project_shapes + edge_shapes + saved_shapes
        if l == 0:
            results = call(
                partial(first_kernel, groups=groups, heads=heads, tok=tok), "layer_first",
                [SMEM] + [spec()] * 13, out_shapes + [bf(layers, ext, lanes)],
                [pltpu.VMEM((ext, feat), BF16), pltpu.VMEM((table_count * tok, 128), F32)],
                group, tables, x, q, kv, gate, from_a, from_b, hot, khot, *weights,
            )
            tsel = results[11]
        else:
            results = call(
                partial(middle_kernel, groups=groups, heads=heads, l=l), "layer_middle",
                [SMEM] + [spec()] * 12, out_shapes, [],
                group, x, q, kv, gate, from_a, from_b, hot, tsel, *weights,
            )
        kvx, w, mixed, residual, up = results[6:11]
        saved.append((x, (q, kvx, w, mixed, gate, residual, up)))
        x, q, kv, gate, to_a, to_b = results[:6]
        from_a, from_b = swapped(to_a, to_b, groups)

    rows_a = (feat * feat + 2 * feat * hidden + hidden * feat) // 128
    rows_q = 4 * feat * feat // 128
    grad_rows = layers * (rows_a + rows_q)
    unit = 16 * groups
    padded = -(-grad_rows // unit) * unit
    back_shapes = [
        shape(atom_dev, feat), bf(atom_dev, feat), bf(atom_dev, feat), shape(atom_dev, 2 * feat)
    ] + edge_shapes
    dkv_scratch = pltpu.VMEM((ext, 2 * feat), F32)
    total_scratch = pltpu.VMEM((atom_dev, 2 * feat), F32)
    l = layers - 1
    results = call(
        partial(turn_kernel, groups=groups, heads=heads, l=l, used=grad_rows), "layer_turn", [SMEM] + [spec()] * 13,
        [bf(atom_dev, feat)] + back_shapes + [shape(heads * tok, span), bf(padded, 128)],
        [pltpu.VMEM(v.shape, v.dtype) for v in saved_shapes] + [dkv_scratch],
        group, x, q, kv, gate, from_a, from_b, hot, khot, tsel, cotangent, *weights[1:],
    )
    out_atoms = results[0]
    d_res, d_q, d_g, center, to_a, to_b, d_t, grads = results[1:]
    d_tables = [d_t]
    row = rows_a
    for l in reversed(range(layers - 1)):
        from_a, from_b = swapped(to_a, to_b, groups)
        x_above, x = x, saved[l][0]
        above = d_tables if l == 0 else []
        extra = [
            pltpu.VMEM((table_count * tok, 128), F32), pltpu.VMEM((table_rows, tok * span), F32)
        ] if l == 0 else []
        args = [
            group, d_res, d_q, d_g, center, from_a, from_b, x_above, *saved[l][1], hot, khot, *weights, *above, grads
        ]
        results = call(
            partial(back_kernel, heads=heads, l=l, row=row, tok=tok, above=len(above)), "layer_back",
            [SMEM] + [spec()] * (len(args) - 1),
            back_shapes + [bf(table_rows, tok * span) if l == 0 else shape(heads * tok, span), bf(padded, 128)],
            [dkv_scratch, total_scratch] + extra, *args, aliases={len(args) - 1: len(back_shapes) + 1},
        )
        d_res, d_q, d_g, center, to_a, to_b, d_t, grads = results
        d_tables = [d_t] + d_tables
        row += rows_q + rows_a
    from_a, from_b = swapped(to_a, to_b, groups)
    flats = spread(d_t, "col")
    half = padded // 2
    args = [group, core, d_res, d_q, d_g, center, from_a, from_b, atoms, w_qkvg, grads]
    grad_atoms, send, grads = call(
        partial(last_kernel, row=row), "project_last", [SMEM] * 2 + [spec()] * 9,
        [bf(atom_dev, feat), bf(half, 128), bf(padded, 128)], [total_scratch], *args, aliases={len(args) - 1: 2},
    )

    cores = [(i, i + 1 - 2 * (i % 2)) for i in range(seq_count)]
    same_core = [[i for i in range(groups) if i // col_count % 2 == c] for c in range(2)]
    shard = padded // groups
    got = lax.ppermute(send, "seq", cores)
    parts = call(
        pair_sum_kernel, "core_sum", [SMEM, spec(), spec()], bf(groups // 2, shard, 128), [], core, grads, got
    )
    part = call(shard_sum_kernel, "shard_sum", [spec()], bf(shard, 128), [], swap(parts, axes, same_core))
    grad_pair, pair_w = call(
        partial(pair_back_kernel, tok=tok), "pair_grads", [SMEM, spec(), HBM, spec()],
        [bf(*pair.shape), bf(table_rows, channels)], tile_scratch, place, flats, pair, wt,
    )
    mine = spread(jnp.concatenate([part, pair_w], axis=0), axes, same_core)
    other = lax.ppermute(mine, "seq", cores)
    scale = 1.0 / math.sqrt(atom_dev * groups)
    *outs, grad_w = call(
        partial(unpack_kernel, scale=scale, height=shard), "unpack", [SMEM, spec(), spec()],
        [shape(*w.shape) for w in weights] + [shape(table_count, channels)], [], core, mine, other,
    )
    return (out_atoms, grad_atoms, grad_pair, *outs, grad_w.T)


def solution(mesh):
    return jax.shard_map(
        per_device,
        mesh=mesh,
        in_specs=(
            P(("seq", "col"), None),
            P(("seq", "col"), None),
            P(),
            P("seq", "col", None),
            P(),
            P(),
            P(),
            P(),
            P(),
        ),
        out_specs=(
            P(("seq", "col"), None),
            P(("seq", "col"), None),
            P("seq", "col", None),
            P(),
            P(),
            P(),
            P(),
            P(),
        ),
        check_vma=False,
    )
```
